128 devices in a mesh: tm: 16 (over y, x_hi, core), dp: 8 (over x_lo, z).
Axes of the slice: x: 4 (x_hi: 2, x_lo: 2; x = x_hi * 2 + x_lo), y: 4, z: 4, core: 2. Of those that a mesh axis runs over, the one named last changes fastest.
Arguments:
- queries: bfloat16 [8, 12288, 1536], P('dp', 'tm'), may hold values from -256 to 256
- key_states: bfloat16 [8, 12288, 1536], P('dp', 'tm'), may hold values from -4 to 4
- value_states: bfloat16 [8, 12288, 1536], P('dp', 'tm'), may hold values from -6 to 6
- out_grad: bfloat16 [8, 12288, 1536], P('dp', 'tm'), may hold values from -12 to 12
- out_weight: bfloat16 [1536, 1536], P('dp'), may hold values from -0.15625 to 0.15625
- win_time: int32 [8, 32, 3], P('dp', 'tm'), may hold values from -1 to 1, as said below
- win_space: int32 [8, 32, 3], P('dp', 'tm'), may hold values from 0 to 1
- tile_len: int32 [8, 32], P('dp'), may hold values from 192 to 384, as said below
Outputs:
- query_grad: bfloat16 [8, 12288, 1536], P('dp', 'tm')
- key_grad: bfloat16 [8, 12288, 1536], P('dp', 'tm')
- value_grad: bfloat16 [8, 12288, 1536], P('dp', 'tm')
- weight_grad: float32 [1536, 1536], P(('tm', 'dp'))
The draws below stay inside these ranges and needn't reach their ends.
Inputs may be any that keep to these rules, and one draw needn't show every extreme that they name: `win_time`: the 3 tiles that a query tile's further slots name are distinct and never the query tile itself; the offset counts slabs along the loop of 16 slabs. `tile_len`: the valid tokens are the first ones of the tile.
All inputs are finite; a program needn't handle non-finite values.
Results may differ from the reference program's by a relative error of at most 0.015.
Values may be sent and summed in bfloat16 or wider, within the bound.
No kernel may reach another device: no remote copies, remote signals or barrier semaphores. Data moves between devices by JAX's collectives and lax.ppermute only.
A program may use at most 192 MiB of HBM per device.

```python
import math
import jax
import jax.numpy as jnp
from jax import lax

HEAD = 128
DOUT = 1536
TILE = 384
W = 4
TPD = 2
HD = 1536
CLIPS = 8
TOKENS = 12288
N_TM = 16


def shared_keys(key):
    base = jnp.clip(jax.random.normal(jax.random.fold_in(key, 1), (CLIPS, TOKENS, HD), jnp.float32), -4.0, 4.0)
    return base


def window_codes(key):
    tile_total = TOKENS // TILE
    pool_count = 3 * TPD
    shape = (CLIPS, tile_total, pool_count)
    slot_id = lax.broadcasted_iota(jnp.int32, shape, 2)
    tile_id = lax.broadcasted_iota(jnp.int32, shape, 1)
    clip_id = lax.broadcasted_iota(jnp.int32, shape, 0)
    ranked = jax.random.randint(jax.random.fold_in(key, 7), shape, 0, 65536) * pool_count + slot_id
    ranked = jnp.where(slot_id == TPD + tile_id % TPD, 2 ** 30, ranked)
    first = (clip_id == 0) & (tile_id == 0)
    ranked = jnp.where(first & (slot_id == 0), -3, ranked)
    ranked = jnp.where(first & (slot_id == 2 * TPD), -2, ranked)
    ranked = jnp.where(first & (slot_id == 3 * TPD - 1), -1, ranked)
    ordered = jnp.argsort(ranked, axis=2, stable=True)
    return ordered[:, :, :W - 1].astype(jnp.int32)


def draw_queries(key, part):
    key = jax.random.fold_in(key, 22)
    own = jnp.clip(2.0 * jax.random.normal(key, (CLIPS, TOKENS, HD), jnp.float32), -8.0, 8.0)
    return own.astype(jnp.bfloat16)


def draw_key_states(key, part):
    base = shared_keys(key)
    return base.astype(jnp.bfloat16)


def draw_win_time(key, part):
    ordered = window_codes(key)
    return (ordered // TPD - 1).astype(jnp.int32)


def draw_win_space(key, part):
    ordered = window_codes(key)
    return (ordered % TPD).astype(jnp.int32)


def draw_tile_len(key, part):
    key = jax.random.fold_in(key, 31)
    shape = (CLIPS, TOKENS // TILE)
    lengths = jax.random.randint(key, shape, TILE // 2, TILE + 1)
    position = lax.broadcasted_iota(jnp.int32, shape, 1)
    lengths = jnp.where(position == 0, TILE, lengths)
    lengths = jnp.where(position == 1, TILE // 2, lengths)
    return lengths.astype(jnp.int32)


def spiked(values, rng, source, target, shards_of, factor):
    owner, partner = [(jnp.arange(values.shape[axis_at]) // (values.shape[axis_at] // shards_of)).reshape([-1 if axis == axis_at else 1 for axis in range(values.ndim)]) for axis_at in (source, target)]
    chosen = jax.random.permutation(rng, shards_of)[partner]
    strong = (owner == chosen) | (owner == (partner + shards_of // 2) % shards_of)
    return jnp.where(strong, factor * values, values)


def block_scale(rng, shape, cuts, least, largest):
    def one(dim, shards_of):
        heights = jax.random.uniform(jax.random.fold_in(jax.random.fold_in(rng, 6), dim), (shards_of,), jnp.float32, least / len(cuts), largest / len(cuts))
        return jnp.repeat(jnp.exp(heights), shape[dim] // shards_of).reshape((-1,) + (1,) * (len(shape) - dim - 1))

    gain = one(*cuts[0])
    for cut in cuts[1:]:
        gain = gain * one(*cut)
    return gain


def centred(stream_key, shape, deviation, limit, split=(), kind=jnp.bfloat16):
    factor_of = block_scale(stream_key, shape, split, -0.22, 0.18) if split else 1.0
    entries = jax.random.normal(stream_key, shape, jnp.float32) * deviation * factor_of
    return jnp.minimum(jnp.maximum(entries, -limit), limit).astype(kind)


def bell_draw_with(own_key, dims, width, reach, shards, heavy, held_as=jnp.bfloat16):
    result = width * jax.random.normal(own_key, dims, jnp.float32)
    if shards:
        result = result * block_scale(own_key, dims, shards, -0.22, 0.18)
    return jnp.clip(spiked(result, jax.random.fold_in(own_key, 3), *heavy), -reach, reach).astype(held_as)


def setup_inputs(seed: int = 0) -> dict:
    seeds = jax.random.split(jax.random.key(seed), 9)
    return {
        "queries": draw_queries(jax.random.fold_in(seeds[8], 71), 0),
        "key_states": draw_key_states(jax.random.fold_in(seeds[8], 71), 0),
        "value_states": centred(seeds[2], (CLIPS, TOKENS, HD), 1.0, 6.0, ((0, 8), (1, 16))),
        "out_grad": bell_draw_with(seeds[3], (CLIPS, TOKENS, DOUT), 2.0, 12.0, ((0, 8), (1, 16)), (1, 2, 16, 2.0)),
        "out_weight": centred(seeds[4], (DOUT, HD), DOUT ** -0.5, 0.15625, ((0, 8),)),
        "win_time": draw_win_time(jax.random.fold_in(seeds[8], 71), 0),
        "win_space": draw_win_space(jax.random.fold_in(seeds[8], 71), 0),
        "tile_len": draw_tile_len(jax.random.fold_in(seeds[8], 71), 0),
    }


def slab_grads(query_tiles, dout_tiles, pool_key, pool_value, pool_len, slot_codes):
    tile_count, tile_size, features = query_tiles.shape
    pool_count = pool_key.shape[0]
    slot_count = slot_codes.shape[1]
    head_count = features // HEAD
    scaling = 1.0 / math.sqrt(HEAD)
    select = slot_codes[:, :, None] == lax.broadcasted_iota(jnp.int32, (tile_count, slot_count, pool_count), 2)
    lengths = lax.optimization_barrier(jnp.sum(jnp.where(select, pool_len[None, None, :], 0), axis=2))
    usable = lax.broadcasted_iota(jnp.int32, (tile_count, slot_count, tile_size), 2) < lengths[:, :, None]
    usable = usable.reshape(tile_count, 1, slot_count * tile_size)
    flat_codes = slot_codes.reshape(-1)
    window_key = jnp.take(pool_key, flat_codes, axis=0).reshape(tile_count, slot_count * tile_size, head_count, HEAD)
    window_value = jnp.take(pool_value, flat_codes, axis=0).reshape(tile_count, slot_count * tile_size, head_count, HEAD)
    select_f = select.astype(jnp.float32)

    def per_head(stacked):
        query_head, dout_head, key_head, value_head = stacked
        query_f = query_head.astype(jnp.float32)
        dout_f = dout_head.astype(jnp.float32)
        key_f = key_head.astype(jnp.float32)
        value_f = value_head.astype(jnp.float32)
        scores = jnp.einsum('tqd,tkd->tqk', query_f, key_f) * scaling
        scores = jnp.where(usable, scores, -jnp.inf)
        row_max = lax.optimization_barrier(jnp.max(scores, axis=2, keepdims=True))
        exponent = jnp.exp(scores - row_max)
        probs_f = exponent / lax.optimization_barrier(jnp.sum(exponent, axis=2, keepdims=True))
        weights = probs_f.astype(jnp.bfloat16)
        weights_f = weights.astype(jnp.float32)
        attended = jnp.einsum('tqk,tkd->tqd', weights_f, value_f).astype(jnp.bfloat16)
        attended = lax.optimization_barrier(attended)
        prob_grad = jnp.einsum('tqd,tkd->tqk', dout_f, value_f)
        rowdot = lax.optimization_barrier(jnp.sum(dout_f * attended.astype(jnp.float32), axis=2, keepdims=True))
        dscore = (probs_f * (prob_grad - rowdot)).astype(jnp.bfloat16)
        dscore_f = dscore.astype(jnp.float32)
        query_out = (jnp.einsum('tqk,tkd->tqd', dscore_f, key_f) * scaling).astype(jnp.bfloat16)
        key_part = jnp.einsum('tqk,tqd->tkd', dscore_f, query_f) * scaling
        value_part = jnp.einsum('tqk,tqd->tkd', weights_f, dout_f)
        key_pool = jnp.einsum('tsp,tskd->pkd', select_f, key_part.reshape(tile_count, slot_count, tile_size, HEAD), precision=lax.Precision.HIGHEST)
        value_pool = jnp.einsum('tsp,tskd->pkd', select_f, value_part.reshape(tile_count, slot_count, tile_size, HEAD), precision=lax.Precision.HIGHEST)
        return (query_out, attended, key_pool, value_pool)
    heads_first = (jnp.moveaxis(query_tiles.reshape(tile_count, tile_size, head_count, HEAD), 2, 0), jnp.moveaxis(dout_tiles.reshape(tile_count, tile_size, head_count, HEAD), 2, 0), jnp.moveaxis(window_key, 2, 0), jnp.moveaxis(window_value, 2, 0))
    query_out, attended, key_pool, value_pool = lax.map(per_head, heads_first)
    query_out = jnp.moveaxis(query_out, 0, 2).reshape(tile_count, tile_size, features)
    attended = jnp.moveaxis(attended, 0, 2).reshape(tile_count, tile_size, features)
    key_pool = jnp.moveaxis(key_pool, 0, 2).reshape(pool_count, tile_size, features)
    value_pool = jnp.moveaxis(value_pool, 0, 2).reshape(pool_count, tile_size, features)
    return (query_out, attended, key_pool, value_pool)

def reference(queries, key_states, value_states, out_grad, out_weight, win_time, win_space, tile_len):
    clip_count, token_count, features = queries.shape
    out_width = out_grad.shape[2]
    slab_count = N_TM
    tile_count = token_count // slab_count // TILE
    head_grad = jnp.dot(out_grad.reshape(-1, out_width), out_weight, preferred_element_type=jnp.float32).astype(jnp.bfloat16)
    tiled_shape = (clip_count, slab_count, tile_count, TILE, features)
    query_tiles = queries.reshape(tiled_shape)
    dout_tiles = head_grad.reshape(tiled_shape)
    key_tiles = key_states.reshape(tiled_shape)
    value_tiles = value_states.reshape(tiled_shape)
    len_tiles = tile_len.reshape(clip_count, slab_count, tile_count)
    time_tiles = win_time.reshape(clip_count, slab_count, tile_count, -1)
    space_tiles = win_space.reshape(clip_count, slab_count, tile_count, -1)
    centre = tile_count + lax.broadcasted_iota(jnp.int32, (tile_count, 1), 0)

    def item_grads(item_index):
        clip_index = item_index // slab_count
        slab_index = item_index % slab_count
        before = (slab_index + slab_count - 1) % slab_count
        later = (slab_index + 1) % slab_count
        pool_key = jnp.concatenate((key_tiles[clip_index, before], key_tiles[clip_index, slab_index], key_tiles[clip_index, later]), axis=0)
        pool_value = jnp.concatenate((value_tiles[clip_index, before], value_tiles[clip_index, slab_index], value_tiles[clip_index, later]), axis=0)
        pool_len = jnp.concatenate((len_tiles[clip_index, before], len_tiles[clip_index, slab_index], len_tiles[clip_index, later]), axis=0)
        further = (time_tiles[clip_index, slab_index] + 1) * tile_count + space_tiles[clip_index, slab_index]
        slot_codes = jnp.concatenate((centre, further), axis=1).astype(jnp.int32)
        query_out, attended, key_pool, value_pool = slab_grads(query_tiles[clip_index, slab_index], dout_tiles[clip_index, slab_index], pool_key, pool_value, pool_len, slot_codes)
        return (query_out, attended, key_pool[tile_count:2 * tile_count], value_pool[tile_count:2 * tile_count], key_pool[:tile_count].astype(jnp.bfloat16), value_pool[:tile_count].astype(jnp.bfloat16), key_pool[2 * tile_count:].astype(jnp.bfloat16), value_pool[2 * tile_count:].astype(jnp.bfloat16))
    items = jnp.arange(clip_count * slab_count, dtype=jnp.int32)
    results = lax.map(item_grads, items)
    shaped = [piece_all.reshape(tiled_shape) for piece_all in results]
    query_out, attended, key_own, value_own, key_prev, value_prev, key_next, value_next = shaped
    key_grad = key_own + jnp.roll(key_prev, -1, axis=1).astype(jnp.float32) + jnp.roll(key_next, 1, axis=1).astype(jnp.float32)
    value_grad = value_own + jnp.roll(value_prev, -1, axis=1).astype(jnp.float32) + jnp.roll(value_next, 1, axis=1).astype(jnp.float32)
    weight_grad = jnp.dot(out_grad.reshape(-1, out_width).T, attended.reshape(-1, features), preferred_element_type=jnp.float32)
    full_shape = (clip_count, token_count, features)
    return (query_out.reshape(full_shape), key_grad.astype(jnp.bfloat16).reshape(full_shape), value_grad.astype(jnp.bfloat16).reshape(full_shape), weight_grad)
```

```python
import functools
import math

import jax
import jax.numpy as jnp
from jax import lax
from jax.experimental import pallas as pl
from jax.experimental.pallas import tpu as pltpu
from jax.sharding import PartitionSpec as P

HEAD = 128
TILE = 384
SLOTS = 4
TILES = 2
ROWS = TILES * TILE
HEADS = 12
FEATURES = HEADS * HEAD
POOL = 3 * TILES
SCALING = 1.0 / math.sqrt(HEAD)
LOG2E = math.log2(math.e)
GROUPS = (2, 4, 6)
CALLS = ((0, 0, 2, 0), (1, 0, 4, 0), (2, 0, 4, 1), (2, 4, 2, 2))
VMEM = 48 * 1024 * 1024
F32 = jnp.float32
BF16 = jnp.bfloat16


def nt(a, b):
    return lax.dot_general(a, b, (((1,), (1,)), ((), ())), preferred_element_type=F32)


def nn(a, b):
    return jnp.dot(a, b, preferred_element_type=F32)


def inner_swap(a):
    return lax.ppermute(a, "tm", [(i, i ^ 1) for i in range(16)])


def outer_swap(a):
    return lax.ppermute(
        a, "tm", [(i, (i + 1) % 16 if i % 2 else (i - 1) % 16) for i in range(16)]
    )


def z_shift(a, by):
    return lax.ppermute(a, "dp", [(i, (i // 4) * 4 + (i + by) % 4) for i in range(8)])


def x_low_swap(a):
    return lax.ppermute(a, "dp", [(i, (i + 4) % 8) for i in range(8)])


def y_shift(a, by):
    return lax.ppermute(a, "tm", [(i, (i + 4 * by) % 16) for i in range(16)])


def x_flip(a, flip_high, flip_low):
    pairs = []
    for tm in range(16):
        for dp in range(8):
            to_tm = tm ^ 2 if flip_high else tm
            to_dp = dp ^ 4 if flip_low else dp
            pairs.append((tm * 8 + dp, to_tm * 8 + to_dp))
    return lax.ppermute(a, ("tm", "dp"), pairs)


def project_kernel(place_ref, rows_ref, *refs):
    pieces, out_ref, held, sems = refs[:8], refs[8], refs[9], refs[10]
    z, core = place_ref[0], place_ref[1]
    copies = []
    for index, piece in enumerate(pieces):
        half = core if index < 4 else 1 - core
        source = lax.rem(z - index % 4 + 4, 4)
        for low in range(2):
            row = pl.multiple_of(low * 768 + source * 192 + half * 96, 96)
            copies.append(
                pltpu.make_async_copy(
                    piece.at[low], held.at[pl.ds(row, 96), :], sems.at[index, low]
                )
            )
    for copy in copies:
        copy.start()
    for copy in copies:
        copy.wait()

    @pl.loop(0, FEATURES // 256)
    def _(j):
        cols = pl.ds(pl.multiple_of(j * 256, 256), 256)
        out_ref[:, cols] = nn(rows_ref[...], held[:, cols]).astype(BF16)


def project(place, rows_in, pieces):
    return pl.pallas_call(
        project_kernel,
        out_shape=jax.ShapeDtypeStruct((ROWS, FEATURES), BF16),
        in_specs=[
            pl.BlockSpec(memory_space=pltpu.SMEM),
            pl.BlockSpec(memory_space=pltpu.VMEM),
        ]
        + [pl.BlockSpec(memory_space=pl.ANY)] * 8,
        out_specs=pl.BlockSpec(memory_space=pltpu.VMEM),
        scratch_shapes=[
            pltpu.VMEM((FEATURES, FEATURES), BF16),
            pltpu.SemaphoreType.DMA((8, 2)),
        ],
        compiler_params=pltpu.CompilerParams(vmem_limit_bytes=VMEM),
        cost_estimate=pl.CostEstimate(
            flops=ROWS * FEATURES, bytes_accessed=1_000_000, transcendentals=0
        ),
        name="project",
    )(place, rows_in, *pieces)


def attention_kernel(
    codes_ref, lens_ref, q_ref, g_ref, ko, vo, ki, vi, kvx, *refs
):
    dq_ref, att_ref, own_ref, in_ref, out_ref = refs[-11:-6]
    kp, vp, kt, vt, acck, accv = refs[-6:]
    for tile in range(TILES):
        part = slice(tile * TILE, (tile + 1) * TILE)
        for base, k, v in (
            (0, ko[part, :], vo[part, :]),
            (2, ki[part, :], vi[part, :]),
            (4, kvx[0, part, :], kvx[1, part, :]),
        ):
            kp[base + tile] = k
            vp[base + tile] = v
            kt[base + tile] = k.T
            vt[base + tile] = v.T
    acck[...] = jnp.zeros_like(acck)
    accv[...] = jnp.zeros_like(accv)
    place = lax.broadcasted_iota(jnp.int32, (TILE, TILE), 0)

    @pl.loop(0, TILES)
    def _(tile):
        rows = pl.ds(pl.multiple_of(tile * TILE, TILE), TILE)
        q = q_ref[rows, :]
        g = g_ref[rows, :]
        codes = [codes_ref[tile, slot] for slot in range(SLOTS)]
        scores = []
        for slot in range(SLOTS):
            s = nt(kp[codes[slot]], q) * (SCALING * LOG2E)
            scores.append(jnp.where(place < lens_ref[tile, slot], s, -jnp.inf))
        top = functools.reduce(
            jnp.maximum, [jnp.max(s, axis=0, keepdims=True) for s in scores]
        )
        powers = [jnp.exp2(s - top) for s in scores]
        total = sum(jnp.sum(e, axis=0, keepdims=True) for e in powers)
        inverse = 1.0 / total
        probs = [e * inverse for e in powers]
        weights = [p.astype(BF16) for p in probs]
        att = sum(nn(vt[codes[slot]], weights[slot]) for slot in range(SLOTS)).astype(BF16)
        att_ref[rows, :] = att.T
        rowdot = jnp.sum(g.T.astype(F32) * att.astype(F32), axis=0, keepdims=True)
        dq = jnp.zeros((HEAD, TILE), F32)
        for slot in range(SLOTS):
            code = codes[slot]
            prob_grad = nt(vp[code], g)
            dscore = (probs[slot] * (prob_grad - rowdot)).astype(BF16)
            dq += nn(kt[code], dscore)
            acck[code] += nn(dscore, q)
            accv[code] += nn(weights[slot], g)
        dq_ref[rows, :] = (dq * SCALING).astype(BF16).T

    for tile in range(TILES):
        part = slice(tile * TILE, (tile + 1) * TILE)
        for base, ref in ((0, own_ref), (2, in_ref), (4, out_ref)):
            ref[0, part, :] = (acck[base + tile] * SCALING).astype(ref.dtype)
            ref[1, part, :] = accv[base + tile].astype(ref.dtype)


def attention(codes, lens, q, g, ko, vo, ki, vi, kvx, first, skip, heads, inside, held, width):
    at_head = pl.BlockSpec((ROWS, HEAD), lambda i: (0, first + i))
    pair = pl.BlockSpec((2, ROWS, HEAD), lambda i: (0, 0, skip + i))
    part = pl.BlockSpec((2, ROWS, HEAD), lambda i: (0, 0, inside + i))
    smem = pl.BlockSpec(memory_space=pltpu.SMEM)
    operands = [codes, lens, q, g, ko, vo, ki, vi, kvx]
    in_specs = [smem, smem] + [at_head] * 6 + [pair]
    aliases = {}
    for index, array in enumerate(held):
        if array is not None:
            aliases[len(operands)] = index
            operands.append(array)
            in_specs.append(pl.BlockSpec(memory_space=pl.ANY))
    whole = jax.ShapeDtypeStruct((ROWS, FEATURES), BF16)
    macs = 6 * heads * TILES * TILE * SLOTS * TILE * HEAD
    return pl.pallas_call(
        attention_kernel,
        grid=(heads,),
        out_shape=[
            whole,
            whole,
            jax.ShapeDtypeStruct((2, ROWS, width), F32),
            jax.ShapeDtypeStruct((2, ROWS, width), BF16),
            jax.ShapeDtypeStruct((2, ROWS, width), BF16),
        ],
        in_specs=in_specs,
        out_specs=[at_head, at_head, part, part, part],
        scratch_shapes=[
            pltpu.VMEM((POOL, TILE, HEAD), BF16),
            pltpu.VMEM((POOL, TILE, HEAD), BF16),
            pltpu.VMEM((POOL, HEAD, TILE), BF16),
            pltpu.VMEM((POOL, HEAD, TILE), BF16),
            pltpu.VMEM((POOL, TILE, HEAD), F32),
            pltpu.VMEM((POOL, TILE, HEAD), F32),
        ],
        input_output_aliases=aliases,
        compiler_params=pltpu.CompilerParams(vmem_limit_bytes=VMEM),
        cost_estimate=pl.CostEstimate(
            flops=macs // 64, bytes_accessed=ROWS * width, transcendentals=0
        ),
        name="attention",
    )(*operands)


def finish_kernel(own_ref, in_ref, out_ref, *refs):
    for index, ref in enumerate(refs[-2:]):
        total = own_ref[index] + in_ref[index].astype(F32) + out_ref[index].astype(F32)
        ref[...] = total.astype(BF16)


def finish(own, from_in, from_out, first, held):
    width = own.shape[2]
    step = 256
    pair = pl.BlockSpec((2, ROWS, step), lambda i: (0, 0, i))
    place = pl.BlockSpec((ROWS, step), lambda i: (0, first * HEAD // step + i))
    whole = jax.ShapeDtypeStruct((ROWS, FEATURES), BF16)
    operands = [own, from_in, from_out] + list(held)
    return pl.pallas_call(
        finish_kernel,
        grid=(width // step,),
        out_shape=[whole, whole],
        in_specs=[pair] * 3 + [pl.BlockSpec(memory_space=pl.ANY)] * len(held),
        out_specs=[place, place],
        input_output_aliases={3 + i: i for i in range(len(held))},
        compiler_params=pltpu.CompilerParams(vmem_limit_bytes=VMEM),
        cost_estimate=pl.CostEstimate(
            flops=ROWS * width, bytes_accessed=ROWS * width, transcendentals=0
        ),
        name="finish",
    )(*operands)


def picked(array, axis, index):
    return lax.dynamic_index_in_dim(array, index, axis, keepdims=False)


def weight_kernel(core_ref, rows_ref, att_ref, *refs):
    for base, core in ((0, core_ref[0]), (2, 1 - core_ref[0])):
        rows = rows_ref[pl.ds(pl.multiple_of(core * 96, 96), 96), :]
        for side in range(2):
            cols = slice(side * 768, (side + 1) * 768)
            ref = refs[base + side]
            ref[0] = nn(rows, att_ref[:, cols]).astype(ref.dtype)


def weight_parts(core, rows_t, att):
    block = pl.BlockSpec((1, 96, 768), lambda i: (i, 0, 0))
    return pl.pallas_call(
        weight_kernel,
        grid=(8,),
        out_shape=[
            jax.ShapeDtypeStruct((8, 96, 768), kind) for kind in (F32, F32, BF16, BF16)
        ],
        in_specs=[
            pl.BlockSpec(memory_space=pltpu.SMEM),
            pl.BlockSpec((192, ROWS), lambda i: (i, 0)),
            pl.BlockSpec((ROWS, FEATURES), lambda i: (0, 0)),
        ],
        out_specs=[block] * 4,
        compiler_params=pltpu.CompilerParams(vmem_limit_bytes=VMEM),
        cost_estimate=pl.CostEstimate(
            flops=ROWS * FEATURES, bytes_accessed=1_000_000, transcendentals=0
        ),
        name="weight_parts",
    )(core, rows_t, att)


def axis_sum(held, axis, index, shift):
    got = [shift(picked(held, axis, (index + by) % 4).astype(BF16), by) for by in (1, 2, 3)]
    return picked(held, axis, index) + sum(a.astype(F32) for a in got)


def x_sum(held, tm, dp):
    x_high, x_low = (tm // 2) % 2, dp // 4
    got = []
    for high, low in ((0, 1), (1, 0), (1, 1)):
        to_high = x_high ^ 1 if high else x_high
        to_low = x_low ^ 1 if low else x_low
        block = picked(picked(held, 0, to_high), 0, to_low)
        got.append(x_flip(block.astype(BF16), high, low))
    own = picked(picked(held, 0, x_high), 0, x_low)
    return own + sum(a.astype(F32) for a in got)


def shards(queries, key_states, value_states, out_grad, out_weight, win_time, win_space, tile_len):
    tm, dp = lax.axis_index("tm"), lax.axis_index("dp")
    core, z = tm % 2, dp % 4
    q, k, v, rows_in = queries[0], key_states[0], value_states[0], out_grad[0]

    step = jnp.concatenate((jnp.zeros((TILES, 1), jnp.int32), win_time[0]), axis=1)
    own = lax.broadcasted_iota(jnp.int32, (TILES, 1), 0)
    space = jnp.concatenate((own, win_space[0]), axis=1)
    to_inner = (step == 1) == (core == 0)
    codes = jnp.where(step == 0, 0, jnp.where(to_inner, 2, 4)) + space
    named = ((tm + step + 16) % 16) * TILES + space
    chosen = named[:, :, None] == lax.broadcasted_iota(jnp.int32, (TILES, SLOTS, 32), 2)
    lens = jnp.sum(jnp.where(chosen, tile_len[0][None, None, :], 0), axis=2)

    starts = [sum(GROUPS[:i]) for i in range(len(GROUPS))]
    together = lax.optimization_barrier

    def outgoing(i):
        cols = slice(starts[i] * HEAD, (starts[i] + GROUPS[i]) * HEAD)
        return jnp.stack((k[:, cols], v[:, cols]))

    x_low = dp // 4
    half = lax.dynamic_slice_in_dim(out_weight, core * 96, 96, 0)
    leaving = [outgoing(i) for i in range(len(GROUPS))]
    other = x_low_swap(half)
    leaving[0], other = together((leaving[0], other))
    arriving = [outer_swap(leaving[0])]
    both = jnp.stack((jnp.where(x_low == 0, half, other), jnp.where(x_low == 0, other, half)))
    mine = [both] + [z_shift(both, by) for by in (1, 2, 3)]
    leaving[1], mine[1] = together((leaving[1], mine[1]))
    arriving.append(outer_swap(leaving[1]))
    leaving[2], arriving[0] = together((leaving[2], arriving[0]))
    arriving.append(outer_swap(leaving[2]))
    ki, vi = inner_swap(k), inner_swap(v)
    ready, arriving[0] = together((tuple(mine), arriving[0]))
    theirs = [inner_swap(a) for a in ready]
    rows_t = together(together((rows_in, both))[0].T)
    place = jnp.stack((z, core)).astype(jnp.int32)
    place, arriving[1] = together((place, arriving[1]))
    head_grad = project(place, rows_in, mine + theirs)


    held = [None] * 5
    inside, first, parts, firsts = 0, 0, [], []
    for group, skip, heads, which in CALLS:
        width = sum(call[2] for call in CALLS if call[3] == which) * HEAD
        held = attention(
            codes, lens, q, head_grad, k, v, ki, vi, arriving[group],
            first, skip, heads, inside, held, width,
        )
        inside += heads
        first += heads
        if inside * HEAD == width:
            parts.append((held[2], inner_swap(held[3]), outer_swap(held[4])))
            firsts.append(first - inside)
            held = list(held[:2]) + [None] * 3
            inside = 0
    dq, att = held[:2]
    keep_a, keep_b, send_a, send_b = weight_parts(place[1:], rows_t, att)
    own, from_in, from_out = parts[0]
    send_a, send_b, from_out = together((send_a, send_b, from_out))
    parts[0] = (own, from_in, from_out)
    y = tm // 4
    late = (keep_b + inner_swap(send_b).astype(F32)).reshape(4, 2, 2, 4, 12, 768)
    early = (keep_a + inner_swap(send_a).astype(F32)).reshape(4, 2, 96, 768)
    early = axis_sum(early, 0, y, y_shift).reshape(2, 2, 4, 12, 768)
    late = axis_sum(late, 3, z, z_shift)
    own, from_in, from_out = parts[1]
    early, late, from_out = together((early, late, from_out))
    parts[1] = (own, from_in, from_out)
    early = axis_sum(early, 2, z, z_shift)
    late = axis_sum(late, 0, y, y_shift)
    own, from_in, from_out = parts[2]
    early, late, from_out = together((early, late, from_out))
    parts[2] = (own, from_in, from_out)
    weight_grad = x_sum(jnp.concatenate((early, late), axis=3), tm, dp)
    grads = ()
    for part, first in zip(parts, firsts):
        grads = finish(*part, first, grads)
    dk, dv = grads
    return dq[None], dk[None], dv[None], weight_grad


def solution(mesh):
    tokens = P("dp", "tm", None)
    in_specs = (tokens, tokens, tokens, tokens, P("dp", None), tokens, tokens, P("dp", None))
    out_specs = (tokens, tokens, tokens, P(("tm", "dp"), None))
    return jax.shard_map(shards, mesh=mesh, in_specs=in_specs, out_specs=out_specs, check_vma=False)
```

```python
import functools
import math

import jax
import jax.numpy as jnp
from jax import lax
from jax.experimental import pallas as pl
from jax.experimental.pallas import tpu as pltpu
from jax.sharding import PartitionSpec as P

HEAD = 128
TILE = 384
SLOTS = 4
TILES = 2
ROWS = TILES * TILE
HEADS = 12
FEATURES = HEADS * HEAD
POOL = 3 * TILES
HALF = FEATURES // 2
SCALING = 1.0 / math.sqrt(HEAD)
LOG2E = math.log2(math.e)
GROUPS = (2, 4, 6)
CALLS = ((0, 0, 2, 0), (1, 0, 4, 0), (2, 0, 6, 1))
VMEM = 48 * 1024 * 1024
F32 = jnp.float32
BF16 = jnp.bfloat16


def nt(a, b):
    return lax.dot_general(a, b, (((1,), (1,)), ((), ())), preferred_element_type=F32)


def nn(a, b):
    return jnp.dot(a, b, preferred_element_type=F32)


def inner_swap(a):
    return lax.ppermute(a, "tm", [(i, i ^ 1) for i in range(16)])


def outer_swap(a):
    return lax.ppermute(
        a, "tm", [(i, (i + 1) % 16 if i % 2 else (i - 1) % 16) for i in range(16)]
    )


def z_shift(a, by):
    return lax.ppermute(a, "dp", [(i, (i // 4) * 4 + (i + by) % 4) for i in range(8)])


def x_low_swap(a):
    return lax.ppermute(a, "dp", [(i, (i + 4) % 8) for i in range(8)])


def y_shift(a, by):
    return lax.ppermute(a, "tm", [(i, (i + 4 * by) % 16) for i in range(16)])


def x_flip(a, flip_high, flip_low):
    pairs = []
    for tm in range(16):
        for dp in range(8):
            to_tm = tm ^ 2 if flip_high else tm
            to_dp = dp ^ 4 if flip_low else dp
            pairs.append((tm * 8 + dp, to_tm * 8 + to_dp))
    return lax.ppermute(a, ("tm", "dp"), pairs)


def project_kernel(place_ref, rows_ref, *refs):
    pieces, out_ref, held, sems = refs[:8], refs[8], refs[9], refs[10]
    z, core = place_ref[0], place_ref[1]
    copies = []
    for index, piece in enumerate(pieces):
        half = core if index < 4 else 1 - core
        source = lax.rem(z - index % 4 + 4, 4)
        for low in range(2):
            row = pl.multiple_of(low * 768 + source * 192 + half * 96, 96)
            copies.append(
                pltpu.make_async_copy(
                    piece.at[low], held.at[pl.ds(row, 96), :], sems.at[index, low]
                )
            )
    for copy in copies:
        copy.start()
    for copy in copies:
        copy.wait()

    @pl.loop(0, FEATURES // 256)
    def _(j):
        cols = pl.ds(pl.multiple_of(j * 256, 256), 256)
        out_ref[:, cols] = nn(rows_ref[...], held[:, cols]).astype(BF16)


def project(place, rows_in, pieces):
    return pl.pallas_call(
        project_kernel,
        out_shape=jax.ShapeDtypeStruct((ROWS, FEATURES), BF16),
        in_specs=[
            pl.BlockSpec(memory_space=pltpu.SMEM),
            pl.BlockSpec(memory_space=pltpu.VMEM),
        ]
        + [pl.BlockSpec(memory_space=pl.ANY)] * 8,
        out_specs=pl.BlockSpec(memory_space=pltpu.VMEM),
        scratch_shapes=[
            pltpu.VMEM((FEATURES, FEATURES), BF16),
            pltpu.SemaphoreType.DMA((8, 2)),
        ],
        compiler_params=pltpu.CompilerParams(vmem_limit_bytes=VMEM),
        cost_estimate=pl.CostEstimate(
            flops=ROWS * FEATURES, bytes_accessed=1_000_000, transcendentals=0
        ),
        name="project",
    )(place, rows_in, *pieces)


def attention_kernel(
    codes_ref, lens_ref, q_ref, g_ref, ko, vo, ki, vi, kvx, *refs
):
    dq_ref, att_ref, own_ref, in_ref, out_ref = refs[-11:-6]
    kp, vp, kt, vt, acck, accv = refs[-6:]
    for tile in range(TILES):
        part = slice(tile * TILE, (tile + 1) * TILE)
        for base, k, v in (
            (0, ko[part, :], vo[part, :]),
            (2, ki[part, :], vi[part, :]),
            (4, kvx[0, part, :], kvx[1, part, :]),
        ):
            kp[base + tile] = k
            vp[base + tile] = v
            kt[base + tile] = k.T
            vt[base + tile] = v.T
    acck[...] = jnp.zeros_like(acck)
    accv[...] = jnp.zeros_like(accv)
    place = lax.broadcasted_iota(jnp.int32, (TILE, TILE), 0)

    for tile in range(TILES):
        rows = slice(tile * TILE, (tile + 1) * TILE)
        q = q_ref[rows, :]
        g = g_ref[rows, :]
        codes = [codes_ref[tile, slot] for slot in range(SLOTS)]
        scores = []
        for slot in range(SLOTS):
            s = nt(kp[codes[slot]], q) * (SCALING * LOG2E)
            scores.append(jnp.where(place < lens_ref[tile, slot], s, -jnp.inf))
        top = functools.reduce(
            jnp.maximum, [jnp.max(s, axis=0, keepdims=True) for s in scores]
        )
        powers = [jnp.exp2(s - top) for s in scores]
        total = sum(jnp.sum(e, axis=0, keepdims=True) for e in powers)
        inverse = 1.0 / total
        probs = [e * inverse for e in powers]
        weights = [p.astype(BF16) for p in probs]
        att = sum(nn(vt[codes[slot]], weights[slot]) for slot in range(SLOTS)).astype(BF16)
        att_ref[rows, :] = att.T
        rowdot = jnp.sum(g.T.astype(F32) * att.astype(F32), axis=0, keepdims=True)
        dq = jnp.zeros((HEAD, TILE), F32)
        for slot in range(SLOTS):
            code = codes[slot]
            prob_grad = nt(vp[code], g)
            dscore = (probs[slot] * (prob_grad - rowdot)).astype(BF16)
            dq += nn(kt[code], dscore)
            acck[code] += nn(dscore, q)
            accv[code] += nn(weights[slot], g)
        dq_ref[rows, :] = (dq * SCALING).astype(BF16).T

    for tile in range(TILES):
        part = slice(tile * TILE, (tile + 1) * TILE)
        for base, ref in ((0, own_ref), (2, in_ref), (4, out_ref)):
            ref[0, part, :] = (acck[base + tile] * SCALING).astype(ref.dtype)
            ref[1, part, :] = accv[base + tile].astype(ref.dtype)


def attention(codes, lens, q, g, ko, vo, ki, vi, kvx, first, skip, heads, inside, held, width):
    at_head = pl.BlockSpec((ROWS, HEAD), lambda i: (0, first + i))
    pair = pl.BlockSpec((2, ROWS, HEAD), lambda i: (0, 0, skip + i))
    part = pl.BlockSpec((2, ROWS, HEAD), lambda i: (0, 0, inside + i))
    smem = pl.BlockSpec(memory_space=pltpu.SMEM)
    operands = [codes, lens, q, g, ko, vo, ki, vi, kvx]
    in_specs = [smem, smem] + [at_head] * 6 + [pair]
    aliases = {}
    for index, array in enumerate(held):
        if array is not None:
            aliases[len(operands)] = index
            operands.append(array)
            in_specs.append(pl.BlockSpec(memory_space=pl.ANY))
    at_half = pl.BlockSpec((ROWS, HEAD), lambda i: (0, first % 6 + i))
    macs = 6 * heads * TILES * TILE * SLOTS * TILE * HEAD
    return pl.pallas_call(
        attention_kernel,
        grid=(heads,),
        out_shape=[
            jax.ShapeDtypeStruct((ROWS, FEATURES), BF16),
            jax.ShapeDtypeStruct((ROWS, HALF), BF16),
            jax.ShapeDtypeStruct((2, ROWS, width), F32),
            jax.ShapeDtypeStruct((2, ROWS, width), BF16),
            jax.ShapeDtypeStruct((2, ROWS, width), BF16),
        ],
        in_specs=in_specs,
        out_specs=[at_head, at_half, part, part, part],
        scratch_shapes=[
            pltpu.VMEM((POOL, TILE, HEAD), BF16),
            pltpu.VMEM((POOL, TILE, HEAD), BF16),
            pltpu.VMEM((POOL, HEAD, TILE), BF16),
            pltpu.VMEM((POOL, HEAD, TILE), BF16),
            pltpu.VMEM((POOL, TILE, HEAD), F32),
            pltpu.VMEM((POOL, TILE, HEAD), F32),
        ],
        input_output_aliases=aliases,
        compiler_params=pltpu.CompilerParams(vmem_limit_bytes=VMEM),
        cost_estimate=pl.CostEstimate(
            flops=macs // 64, bytes_accessed=ROWS * width, transcendentals=0
        ),
        name="attention",
    )(*operands)


def finish_kernel(own_ref, in_ref, out_ref, *refs):
    for index, ref in enumerate(refs[-2:]):
        total = own_ref[index] + in_ref[index].astype(F32) + out_ref[index].astype(F32)
        ref[...] = total.astype(BF16)


def finish(own, from_in, from_out, first, held):
    width = own.shape[2]
    step = 256
    pair = pl.BlockSpec((2, ROWS, step), lambda i: (0, 0, i))
    place = pl.BlockSpec((ROWS, step), lambda i: (0, first * HEAD // step + i))
    whole = jax.ShapeDtypeStruct((ROWS, FEATURES), BF16)
    operands = [own, from_in, from_out] + list(held)
    return pl.pallas_call(
        finish_kernel,
        grid=(width // step,),
        out_shape=[whole, whole],
        in_specs=[pair] * 3 + [pl.BlockSpec(memory_space=pl.ANY)] * len(held),
        out_specs=[place, place],
        input_output_aliases={3 + i: i for i in range(len(held))},
        compiler_params=pltpu.CompilerParams(vmem_limit_bytes=VMEM),
        cost_estimate=pl.CostEstimate(
            flops=ROWS * width, bytes_accessed=ROWS * width, transcendentals=0
        ),
        name="finish",
    )(*operands)


def picked(array, axis, index):
    return lax.dynamic_index_in_dim(array, index, axis, keepdims=False)


def weight_kernel(core_ref, rows_ref, att_ref, keep_ref, send_ref):
    for ref, core in ((keep_ref, core_ref[0]), (send_ref, 1 - core_ref[0])):
        rows = rows_ref[pl.ds(pl.multiple_of(core * 96, 96), 96), :]
        ref[0] = nn(rows, att_ref[...]).astype(ref.dtype)


def weight_parts(core, rows_t, att):
    block = pl.BlockSpec((1, 96, HALF), lambda i: (i, 0, 0))
    return pl.pallas_call(
        weight_kernel,
        grid=(8,),
        out_shape=[jax.ShapeDtypeStruct((8, 96, HALF), kind) for kind in (F32, BF16)],
        in_specs=[
            pl.BlockSpec(memory_space=pltpu.SMEM),
            pl.BlockSpec((192, ROWS), lambda i: (i, 0)),
            pl.BlockSpec((ROWS, HALF), lambda i: (0, 0)),
        ],
        out_specs=[block, block],
        compiler_params=pltpu.CompilerParams(vmem_limit_bytes=VMEM),
        cost_estimate=pl.CostEstimate(
            flops=ROWS * HALF, bytes_accessed=500_000, transcendentals=0
        ),
        name="weight_parts",
    )(core, rows_t, att)


def core_sum_kernel(z_ref, keep_ref, got_ref, *refs):
    held = refs[4]
    for high in range(2):
        total = keep_ref[high] + got_ref[high].astype(F32)
        for low in range(2):
            for z in range(4):
                row, place = low * 48 + z * 12, (high * 2 + low) * 12
                by = lax.rem(z - z_ref[0] + 4, 4)
                held[by, place : place + 12, :] = total[row : row + 12, :]
    for by, ref in enumerate(refs[:4]):
        ref[...] = held[by].astype(ref.dtype)


def core_sum(z, keep, got):
    block = pl.BlockSpec((2, 96, HALF), lambda i: (i, 0, 0))
    return pl.pallas_call(
        core_sum_kernel,
        grid=(4,),
        out_shape=[jax.ShapeDtypeStruct((192, HALF), kind) for kind in (F32, BF16, BF16, BF16)],
        in_specs=[pl.BlockSpec(memory_space=pltpu.SMEM), block, block],
        out_specs=[pl.BlockSpec((48, HALF), lambda i: (i, 0))] * 4,
        scratch_shapes=[pltpu.VMEM((4, 48, HALF), F32)],
        compiler_params=pltpu.CompilerParams(vmem_limit_bytes=VMEM),
        cost_estimate=pl.CostEstimate(
            flops=ROWS * HALF, bytes_accessed=500_000, transcendentals=0
        ),
        name="core_sum",
    )(z, keep, got)


def z_sum_kernel(y_ref, *refs):
    outs, held = refs[8:12], refs[12]
    for side in range(2):
        own, got = refs[4 * side], refs[4 * side + 1 : 4 * side + 4]
        cols = slice(side * HALF, (side + 1) * HALF)
        held[:, cols] = own[...] + sum(ref[...].astype(F32) for ref in got)
    for by, ref in enumerate(outs):
        row = pl.multiple_of(lax.rem(y_ref[0] + by, 4) * 48, 48)
        ref[...] = held[pl.ds(row, 48), :].astype(ref.dtype)


def z_sum(y, sides):
    whole = pl.BlockSpec(memory_space=pltpu.VMEM)
    return pl.pallas_call(
        z_sum_kernel,
        out_shape=[jax.ShapeDtypeStruct((48, FEATURES), kind) for kind in (F32, BF16, BF16, BF16)],
        in_specs=[pl.BlockSpec(memory_space=pltpu.SMEM)] + [whole] * 8,
        out_specs=[whole] * 4,
        scratch_shapes=[pltpu.VMEM((192, FEATURES), F32)],
        compiler_params=pltpu.CompilerParams(vmem_limit_bytes=VMEM),
        cost_estimate=pl.CostEstimate(
            flops=ROWS * HALF, bytes_accessed=500_000, transcendentals=0
        ),
        name="z_sum",
    )(y, *sides)


def x_sum(held, tm, dp):
    x_high, x_low = (tm // 2) % 2, dp // 4
    got = []
    for high, low in ((0, 1), (1, 0), (1, 1)):
        to_high = x_high ^ 1 if high else x_high
        to_low = x_low ^ 1 if low else x_low
        block = picked(picked(held, 0, to_high), 0, to_low)
        got.append(x_flip(block.astype(BF16), high, low))
    own = picked(picked(held, 0, x_high), 0, x_low)
    return own + sum(a.astype(F32) for a in got)


def shards(queries, key_states, value_states, out_grad, out_weight, win_time, win_space, tile_len):
    tm, dp = lax.axis_index("tm"), lax.axis_index("dp")
    core, z = tm % 2, dp % 4
    q, k, v, rows_in = queries[0], key_states[0], value_states[0], out_grad[0]

    step = jnp.concatenate((jnp.zeros((TILES, 1), jnp.int32), win_time[0]), axis=1)
    own = lax.broadcasted_iota(jnp.int32, (TILES, 1), 0)
    space = jnp.concatenate((own, win_space[0]), axis=1)
    to_inner = (step == 1) == (core == 0)
    codes = jnp.where(step == 0, 0, jnp.where(to_inner, 2, 4)) + space
    named = ((tm + step + 16) % 16) * TILES + space
    chosen = named[:, :, None] == lax.broadcasted_iota(jnp.int32, (TILES, SLOTS, 32), 2)
    lens = jnp.sum(jnp.where(chosen, tile_len[0][None, None, :], 0), axis=2)

    starts = [sum(GROUPS[:i]) for i in range(len(GROUPS))]
    together = lax.optimization_barrier

    def outgoing(i):
        cols = slice(starts[i] * HEAD, (starts[i] + GROUPS[i]) * HEAD)
        return jnp.stack((k[:, cols], v[:, cols]))

    x_low = dp // 4
    half = lax.dynamic_slice_in_dim(out_weight, core * 96, 96, 0)
    leaving = [outgoing(i) for i in range(len(GROUPS))]
    other = x_low_swap(half)
    leaving[0], other = together((leaving[0], other))
    arriving = [outer_swap(leaving[0])]
    both = jnp.stack((jnp.where(x_low == 0, half, other), jnp.where(x_low == 0, other, half)))
    mine = [both] + [z_shift(both, by) for by in (1, 2, 3)]
    leaving[1], mine[1] = together((leaving[1], mine[1]))
    arriving.append(outer_swap(leaving[1]))
    leaving[2], arriving[0] = together((leaving[2], arriving[0]))
    arriving.append(outer_swap(leaving[2]))
    ki, vi = inner_swap(k), inner_swap(v)
    rows_t = together((rows_in, both))[0].T
    ready, arriving[0], rows_t = together((tuple(mine), arriving[0], rows_t))
    theirs = [inner_swap(a) for a in ready]
    place = jnp.stack((z, core)).astype(jnp.int32)
    place, arriving[1] = together((place, arriving[1]))
    head_grad = project(place, rows_in, mine + theirs)


    held = [None] * 5
    inside, first, parts, firsts = 0, 0, [], []
    for group, skip, heads, which in CALLS:
        width = sum(call[2] for call in CALLS if call[3] == which) * HEAD
        if first == 6:
            att_a = held[1]
            held = [held[0]] + [None] * 4
        held = attention(
            codes, lens, q, head_grad, k, v, ki, vi, arriving[group],
            first, skip, heads, inside, held, width,
        )
        inside += heads
        first += heads
        if inside * HEAD == width:
            parts.append([held[2], inner_swap(held[3]), outer_swap(held[4])])
            firsts.append(first - inside)
            held = list(held[:2]) + [None] * 3
            inside = 0
    dq, att_b = held[:2]
    att_a, att_b = together((att_a, att_b))
    keep_a, send_a = weight_parts(place[1:], rows_t, att_a)
    sums_a = core_sum(place[:1], keep_a, inner_swap(send_a))
    side_a = [sums_a[0]] + [z_shift(sums_a[by], by) for by in (1, 2, 3)]
    keep_b, send_b = weight_parts(place[1:], rows_t, att_b)
    send_b, parts[0][2] = together((send_b, parts[0][2]))
    sums_b = core_sum(place[:1], keep_b, inner_swap(send_b))
    side_b = [sums_b[0]] + [z_shift(sums_b[by], by) for by in (1, 2, 3)]
    sums = z_sum((tm // 4).astype(jnp.int32)[None], side_a + side_b)
    total = sums[0] + sum(y_shift(sums[by], by).astype(F32) for by in (1, 2, 3))
    grads = finish(*parts[0], 0, ())
    total, parts[1][2], *grads = together((total, parts[1][2], *grads))
    weight_grad = x_sum(total.reshape(2, 2, 12, FEATURES), tm, dp)
    dk, dv = finish(*parts[1], firsts[1], grads)
    return dq[None], dk[None], dv[None], weight_grad


def solution(mesh):
    tokens = P("dp", "tm", None)
    in_specs = (tokens, tokens, tokens, tokens, P("dp", None), tokens, tokens, P("dp", None))
    out_specs = (tokens, tokens, tokens, P(("tm", "dp"), None))
    return jax.shard_map(shards, mesh=mesh, in_specs=in_specs, out_specs=out_specs, check_vma=False)
```

```python
import functools
import math

import jax
import jax.numpy as jnp
from jax import lax
from jax.experimental import pallas as pl
from jax.experimental.pallas import tpu as pltpu
from jax.sharding import PartitionSpec as P

HEAD = 128
TILE = 384
SLOTS = 4
TILES = 2
ROWS = TILES * TILE
HEADS = 12
FEATURES = HEADS * HEAD
POOL = 3 * TILES
HALF = FEATURES // 2
SCALING = 1.0 / math.sqrt(HEAD)
LOG2E = math.log2(math.e)
GROUPS = (2, 4, 6)
CALLS = ((0, 0, 2, 0), (1, 0, 4, 0), (2, 0, 6, 1))
VMEM = 48 * 1024 * 1024
F32 = jnp.float32
BF16 = jnp.bfloat16


def nt(a, b):
    return lax.dot_general(a, b, (((1,), (1,)), ((), ())), preferred_element_type=F32)


def nn(a, b):
    return jnp.dot(a, b, preferred_element_type=F32)


def inner_swap(a):
    return lax.ppermute(a, "tm", [(i, i ^ 1) for i in range(16)])


def outer_swap(a):
    return lax.ppermute(
        a, "tm", [(i, (i + 1) % 16 if i % 2 else (i - 1) % 16) for i in range(16)]
    )


def z_shift(a, by):
    return lax.ppermute(a, "dp", [(i, (i // 4) * 4 + (i + by) % 4) for i in range(8)])


def x_low_swap(a):
    return lax.ppermute(a, "dp", [(i, (i + 4) % 8) for i in range(8)])


def y_shift(a, by):
    return lax.ppermute(a, "tm", [(i, (i + 4 * by) % 16) for i in range(16)])


def x_flip(a, flip_high, flip_low):
    pairs = []
    for tm in range(16):
        for dp in range(8):
            to_tm = tm ^ 2 if flip_high else tm
            to_dp = dp ^ 4 if flip_low else dp
            pairs.append((tm * 8 + dp, to_tm * 8 + to_dp))
    return lax.ppermute(a, ("tm", "dp"), pairs)


def project_kernel(place_ref, rows_ref, *refs):
    pieces, out_ref, held, sems = refs[:8], refs[8], refs[9], refs[10]
    z, core = place_ref[0], place_ref[1]
    copies = []
    for index, piece in enumerate(pieces):
        half = core if index < 4 else 1 - core
        source = lax.rem(z - index % 4 + 4, 4)
        for low in range(2):
            row = pl.multiple_of(low * 768 + source * 192 + half * 96, 96)
            copies.append(
                pltpu.make_async_copy(
                    piece.at[low], held.at[pl.ds(row, 96), :], sems.at[index, low]
                )
            )
    for copy in copies:
        copy.start()
    for copy in copies:
        copy.wait()

    @pl.loop(0, FEATURES // 256)
    def _(j):
        cols = pl.ds(pl.multiple_of(j * 256, 256), 256)
        out_ref[:, cols] = nn(rows_ref[...], held[:, cols]).astype(BF16)


def project(place, rows_in, pieces):
    return pl.pallas_call(
        project_kernel,
        out_shape=jax.ShapeDtypeStruct((ROWS, FEATURES), BF16),
        in_specs=[
            pl.BlockSpec(memory_space=pltpu.SMEM),
            pl.BlockSpec(memory_space=pltpu.VMEM),
        ]
        + [pl.BlockSpec(memory_space=pl.ANY)] * 8,
        out_specs=pl.BlockSpec(memory_space=pltpu.VMEM),
        scratch_shapes=[
            pltpu.VMEM((FEATURES, FEATURES), BF16),
            pltpu.SemaphoreType.DMA((8, 2)),
        ],
        compiler_params=pltpu.CompilerParams(vmem_limit_bytes=VMEM),
        cost_estimate=pl.CostEstimate(
            flops=ROWS * FEATURES, bytes_accessed=1_000_000, transcendentals=0
        ),
        name="project",
    )(place, rows_in, *pieces)


def attention_kernel(
    codes_ref, lens_ref, q_ref, g_ref, ko, vo, ki, vi, kvx, *refs
):
    dq_ref, att_ref, own_ref, in_ref, out_ref = refs[-11:-6]
    kp, vp, kt, vt, acck, accv = refs[-6:]
    for tile in range(TILES):
        part = slice(tile * TILE, (tile + 1) * TILE)
        for base, k, v in (
            (0, ko[part, :], vo[part, :]),
            (2, ki[part, :], vi[part, :]),
            (4, kvx[0, part, :], kvx[1, part, :]),
        ):
            kp[base + tile] = k
            vp[base + tile] = v
            kt[base + tile] = k.T
            vt[base + tile] = v.T
    acck[...] = jnp.zeros_like(acck)
    accv[...] = jnp.zeros_like(accv)
    place = lax.broadcasted_iota(jnp.int32, (TILE, TILE), 0)

    for tile in range(TILES):
        rows = slice(tile * TILE, (tile + 1) * TILE)
        q = q_ref[rows, :]
        g = g_ref[rows, :]
        codes = [codes_ref[tile, slot] for slot in range(SLOTS)]
        scores = []
        for slot in range(SLOTS):
            s = nt(kp[codes[slot]], q) * (SCALING * LOG2E)
            scores.append(jnp.where(place < lens_ref[tile, slot], s, -jnp.inf))
        top = functools.reduce(
            jnp.maximum, [jnp.max(s, axis=0, keepdims=True) for s in scores]
        )
        powers = [jnp.exp2(s - top) for s in scores]
        total = sum(jnp.sum(e, axis=0, keepdims=True) for e in powers)
        inverse = 1.0 / total
        probs = [e * inverse for e in powers]
        weights = [p.astype(BF16) for p in probs]
        every = jnp.concatenate(weights, axis=0)
        att = nn(jnp.concatenate([vt[code] for code in codes], axis=1), every).astype(BF16)
        att_ref[rows, :] = att.T
        rowdot = jnp.sum(g.T.astype(F32) * att.astype(F32), axis=0, keepdims=True)
        dscores = []
        for slot in range(SLOTS):
            code = codes[slot]
            prob_grad = nt(vp[code], g)
            dscore = (probs[slot] * (prob_grad - rowdot)).astype(BF16)
            dscores.append(dscore)
            acck[code] += nn(dscore, q)
            accv[code] += nn(weights[slot], g)
        every = jnp.concatenate(dscores, axis=0)
        dq = nn(jnp.concatenate([kt[code] for code in codes], axis=1), every)
        dq_ref[rows, :] = (dq * SCALING).astype(BF16).T

    for tile in range(TILES):
        part = slice(tile * TILE, (tile + 1) * TILE)
        for base, ref in ((0, own_ref), (2, in_ref), (4, out_ref)):
            ref[0, part, :] = (acck[base + tile] * SCALING).astype(ref.dtype)
            ref[1, part, :] = accv[base + tile].astype(ref.dtype)


def attention(codes, lens, q, g, ko, vo, ki, vi, kvx, first, skip, heads, inside, held, width):
    at_head = pl.BlockSpec((ROWS, HEAD), lambda i: (0, first + i))
    pair = pl.BlockSpec((2, ROWS, HEAD), lambda i: (0, 0, skip + i))
    part = pl.BlockSpec((2, ROWS, HEAD), lambda i: (0, 0, inside + i))
    smem = pl.BlockSpec(memory_space=pltpu.SMEM)
    operands = [codes, lens, q, g, ko, vo, ki, vi, kvx]
    in_specs = [smem, smem] + [at_head] * 6 + [pair]
    aliases = {}
    for index, array in enumerate(held):
        if array is not None:
            aliases[len(operands)] = index
            operands.append(array)
            in_specs.append(pl.BlockSpec(memory_space=pl.ANY))
    at_half = pl.BlockSpec((ROWS, HEAD), lambda i: (0, first % 6 + i))
    macs = 6 * heads * TILES * TILE * SLOTS * TILE * HEAD
    return pl.pallas_call(
        attention_kernel,
        grid=(heads,),
        out_shape=[
            jax.ShapeDtypeStruct((ROWS, FEATURES), BF16),
            jax.ShapeDtypeStruct((ROWS, HALF), BF16),
            jax.ShapeDtypeStruct((2, ROWS, width), F32),
            jax.ShapeDtypeStruct((2, ROWS, width), BF16),
            jax.ShapeDtypeStruct((2, ROWS, width), BF16),
        ],
        in_specs=in_specs,
        out_specs=[at_head, at_half, part, part, part],
        scratch_shapes=[
            pltpu.VMEM((POOL, TILE, HEAD), BF16),
            pltpu.VMEM((POOL, TILE, HEAD), BF16),
            pltpu.VMEM((POOL, HEAD, TILE), BF16),
            pltpu.VMEM((POOL, HEAD, TILE), BF16),
            pltpu.VMEM((POOL, TILE, HEAD), F32),
            pltpu.VMEM((POOL, TILE, HEAD), F32),
        ],
        input_output_aliases=aliases,
        compiler_params=pltpu.CompilerParams(vmem_limit_bytes=VMEM),
        cost_estimate=pl.CostEstimate(
            flops=macs // 64, bytes_accessed=ROWS * width, transcendentals=0
        ),
        name="attention",
    )(*operands)


def finish_kernel(own_ref, in_ref, out_ref, *refs):
    for index, ref in enumerate(refs[-2:]):
        total = own_ref[index] + in_ref[index].astype(F32) + out_ref[index].astype(F32)
        ref[...] = total.astype(BF16)


def finish(own, from_in, from_out, first, held):
    width = own.shape[2]
    step = 256
    pair = pl.BlockSpec((2, ROWS, step), lambda i: (0, 0, i))
    place = pl.BlockSpec((ROWS, step), lambda i: (0, first * HEAD // step + i))
    whole = jax.ShapeDtypeStruct((ROWS, FEATURES), BF16)
    operands = [own, from_in, from_out] + list(held)
    return pl.pallas_call(
        finish_kernel,
        grid=(width // step,),
        out_shape=[whole, whole],
        in_specs=[pair] * 3 + [pl.BlockSpec(memory_space=pl.ANY)] * len(held),
        out_specs=[place, place],
        input_output_aliases={3 + i: i for i in range(len(held))},
        compiler_params=pltpu.CompilerParams(vmem_limit_bytes=VMEM),
        cost_estimate=pl.CostEstimate(
            flops=ROWS * width, bytes_accessed=ROWS * width, transcendentals=0
        ),
        name="finish",
    )(*operands)


def picked(array, axis, index):
    return lax.dynamic_index_in_dim(array, index, axis, keepdims=False)


def weight_kernel(core_ref, rows_ref, att_ref, keep_ref, send_ref, held):
    for part in range(4):
        rows = slice(part * 384, (part + 1) * 384)
        held[2 * part : 2 * part + 2] = nn(rows_ref[rows, :], att_ref[...]).reshape(2, 192, 256)
    for ref, core in ((keep_ref, core_ref[0]), (send_ref, 1 - core_ref[0])):
        rows = pl.ds(pl.multiple_of(core * 96, 96), 96)
        ref[...] = held[:, rows, :].astype(ref.dtype)


def weight_parts(core, rows_t, att):
    block = pl.BlockSpec((8, 96, 256), lambda i: (0, 0, i))
    return pl.pallas_call(
        weight_kernel,
        grid=(HALF // 256,),
        out_shape=[jax.ShapeDtypeStruct((8, 96, HALF), kind) for kind in (F32, BF16)],
        in_specs=[
            pl.BlockSpec(memory_space=pltpu.SMEM),
            pl.BlockSpec((FEATURES, ROWS), lambda i: (0, 0)),
            pl.BlockSpec((ROWS, 256), lambda i: (0, i)),
        ],
        out_specs=[block, block],
        scratch_shapes=[pltpu.VMEM((8, 192, 256), F32)],
        compiler_params=pltpu.CompilerParams(vmem_limit_bytes=VMEM),
        cost_estimate=pl.CostEstimate(
            flops=ROWS * HALF, bytes_accessed=500_000, transcendentals=0
        ),
        name="weight_parts",
    )(core, rows_t, att)


def core_sum_kernel(z_ref, keep_ref, got_ref, *refs):
    held = refs[4]
    for high in range(2):
        total = keep_ref[high] + got_ref[high].astype(F32)
        for low in range(2):
            for z in range(4):
                row, place = low * 48 + z * 12, (high * 2 + low) * 12
                by = lax.rem(z - z_ref[0] + 4, 4)
                held[by, place : place + 12, :] = total[row : row + 12, :]
    for by, ref in enumerate(refs[:4]):
        ref[...] = held[by].astype(ref.dtype)


def core_sum(z, keep, got):
    block = pl.BlockSpec((2, 96, HALF), lambda i: (i, 0, 0))
    return pl.pallas_call(
        core_sum_kernel,
        grid=(4,),
        out_shape=[jax.ShapeDtypeStruct((192, HALF), kind) for kind in (F32, BF16, BF16, BF16)],
        in_specs=[pl.BlockSpec(memory_space=pltpu.SMEM), block, block],
        out_specs=[pl.BlockSpec((48, HALF), lambda i: (i, 0))] * 4,
        scratch_shapes=[pltpu.VMEM((4, 48, HALF), F32)],
        compiler_params=pltpu.CompilerParams(vmem_limit_bytes=VMEM),
        cost_estimate=pl.CostEstimate(
            flops=ROWS * HALF, bytes_accessed=500_000, transcendentals=0
        ),
        name="core_sum",
    )(z, keep, got)


def z_sum_kernel(y_ref, *refs):
    outs, held = refs[8:12], refs[12]
    for side in range(2):
        own, got = refs[4 * side], refs[4 * side + 1 : 4 * side + 4]
        cols = slice(side * HALF, (side + 1) * HALF)
        held[:, cols] = own[...] + sum(ref[...].astype(F32) for ref in got)
    for by, ref in enumerate(outs):
        row = pl.multiple_of(lax.rem(y_ref[0] + by, 4) * 48, 48)
        ref[...] = held[pl.ds(row, 48), :].astype(ref.dtype)


def z_sum(y, sides):
    whole = pl.BlockSpec(memory_space=pltpu.VMEM)
    return pl.pallas_call(
        z_sum_kernel,
        out_shape=[jax.ShapeDtypeStruct((48, FEATURES), kind) for kind in (F32, BF16, BF16, BF16)],
        in_specs=[pl.BlockSpec(memory_space=pltpu.SMEM)] + [whole] * 8,
        out_specs=[whole] * 4,
        scratch_shapes=[pltpu.VMEM((192, FEATURES), F32)],
        compiler_params=pltpu.CompilerParams(vmem_limit_bytes=VMEM),
        cost_estimate=pl.CostEstimate(
            flops=ROWS * HALF, bytes_accessed=500_000, transcendentals=0
        ),
        name="z_sum",
    )(y, *sides)


def x_sum(held, tm, dp):
    x_high, x_low = (tm // 2) % 2, dp // 4
    got = []
    for high, low in ((0, 1), (1, 0), (1, 1)):
        to_high = x_high ^ 1 if high else x_high
        to_low = x_low ^ 1 if low else x_low
        block = picked(picked(held, 0, to_high), 0, to_low)
        got.append(x_flip(block.astype(BF16), high, low))
    own = picked(picked(held, 0, x_high), 0, x_low)
    return own + sum(a.astype(F32) for a in got)


def shards(queries, key_states, value_states, out_grad, out_weight, win_time, win_space, tile_len):
    tm, dp = lax.axis_index("tm"), lax.axis_index("dp")
    core, z = tm % 2, dp % 4
    q, k, v, rows_in = queries[0], key_states[0], value_states[0], out_grad[0]

    step = jnp.concatenate((jnp.zeros((TILES, 1), jnp.int32), win_time[0]), axis=1)
    own = lax.broadcasted_iota(jnp.int32, (TILES, 1), 0)
    space = jnp.concatenate((own, win_space[0]), axis=1)
    to_inner = (step == 1) == (core == 0)
    codes = jnp.where(step == 0, 0, jnp.where(to_inner, 2, 4)) + space
    named = ((tm + step + 16) % 16) * TILES + space
    chosen = named[:, :, None] == lax.broadcasted_iota(jnp.int32, (TILES, SLOTS, 32), 2)
    lens = jnp.sum(jnp.where(chosen, tile_len[0][None, None, :], 0), axis=2)

    starts = [sum(GROUPS[:i]) for i in range(len(GROUPS))]
    together = lax.optimization_barrier

    def outgoing(i):
        cols = slice(starts[i] * HEAD, (starts[i] + GROUPS[i]) * HEAD)
        return jnp.stack((k[:, cols], v[:, cols]))

    x_low = dp // 4
    half = lax.dynamic_slice_in_dim(out_weight, core * 96, 96, 0)
    leaving = [outgoing(i) for i in range(len(GROUPS))]
    other = x_low_swap(half)
    leaving[0], other = together((leaving[0], other))
    arriving = [outer_swap(leaving[0])]
    both = jnp.stack((jnp.where(x_low == 0, half, other), jnp.where(x_low == 0, other, half)))
    mine = [both] + [z_shift(both, by) for by in (1, 2, 3)]
    leaving[1], mine[1] = together((leaving[1], mine[1]))
    arriving.append(outer_swap(leaving[1]))
    leaving[2], arriving[0] = together((leaving[2], arriving[0]))
    arriving.append(outer_swap(leaving[2]))
    ki, vi = inner_swap(k), inner_swap(v)
    rows_t = together((rows_in, both))[0].T
    ready, arriving[0], rows_t = together((tuple(mine), arriving[0], rows_t))
    theirs = [inner_swap(a) for a in ready]
    place = jnp.stack((z, core)).astype(jnp.int32)
    place, arriving[1] = together((place, arriving[1]))
    head_grad = project(place, rows_in, mine + theirs)


    held = [None] * 5
    inside, first, parts, firsts = 0, 0, [], []
    for group, skip, heads, which in CALLS:
        width = sum(call[2] for call in CALLS if call[3] == which) * HEAD
        if first == 6:
            att_a = held[1]
            held = [held[0]] + [None] * 4
        held = attention(
            codes, lens, q, head_grad, k, v, ki, vi, arriving[group],
            first, skip, heads, inside, held, width,
        )
        inside += heads
        first += heads
        if inside * HEAD == width:
            parts.append([held[2], inner_swap(held[3]), outer_swap(held[4])])
            firsts.append(first - inside)
            held = list(held[:2]) + [None] * 3
            inside = 0
    dq, att_b = held[:2]
    att_a, att_b = together((att_a, att_b))
    keep_a, send_a = weight_parts(place[1:], rows_t, att_a)
    sums_a = core_sum(place[:1], keep_a, inner_swap(send_a))
    side_a = [sums_a[0]] + [z_shift(sums_a[by], by) for by in (1, 2, 3)]
    keep_b, send_b = weight_parts(place[1:], rows_t, att_b)
    send_b, parts[0][2] = together((send_b, parts[0][2]))
    sums_b = core_sum(place[:1], keep_b, inner_swap(send_b))
    side_b = [sums_b[0]] + [z_shift(sums_b[by], by) for by in (1, 2, 3)]
    grads = finish(*parts[0], 0, ())
    side_a[0], *grads = together((side_a[0], *grads))
    sums = z_sum((tm // 4).astype(jnp.int32)[None], side_a + side_b)
    total = sums[0] + sum(y_shift(sums[by], by).astype(F32) for by in (1, 2, 3))
    total, parts[1][2] = together((total, parts[1][2]))
    weight_grad = x_sum(total.reshape(2, 2, 12, FEATURES), tm, dp)
    dk, dv = finish(*parts[1], firsts[1], grads)
    return dq[None], dk[None], dv[None], weight_grad


def solution(mesh):
    tokens = P("dp", "tm", None)
    in_specs = (tokens, tokens, tokens, tokens, P("dp", None), tokens, tokens, P("dp", None))
    out_specs = (tokens, tokens, tokens, P(("tm", "dp"), None))
    return jax.shard_map(shards, mesh=mesh, in_specs=in_specs, out_specs=out_specs, check_vma=False)
```

```python
import functools
import math

import jax
import jax.numpy as jnp
from jax import lax
from jax.experimental import pallas as pl
from jax.experimental.pallas import tpu as pltpu
from jax.sharding import PartitionSpec as P

HEAD = 128
TILE = 384
SLOTS = 4
TILES = 2
ROWS = TILES * TILE
HEADS = 12
FEATURES = HEADS * HEAD
POOL = 3 * TILES
HALF = FEATURES // 2
SCALING = 1.0 / math.sqrt(HEAD)
LOG2E = math.log2(math.e)
GROUPS = (2, 4, 6)
CALLS = ((0, 0, 2, 0), (1, 0, 4, 0), (2, 0, 6, 1))
VMEM = 48 * 1024 * 1024
F32 = jnp.float32
BF16 = jnp.bfloat16


def nt(a, b):
    return lax.dot_general(a, b, (((1,), (1,)), ((), ())), preferred_element_type=F32)


def nn(a, b):
    return jnp.dot(a, b, preferred_element_type=F32)


def inner_swap(a):
    return lax.ppermute(a, "tm", [(i, i ^ 1) for i in range(16)])


def outer_swap(a):
    return lax.ppermute(
        a, "tm", [(i, (i + 1) % 16 if i % 2 else (i - 1) % 16) for i in range(16)]
    )


def z_shift(a, by):
    return lax.ppermute(a, "dp", [(i, (i // 4) * 4 + (i + by) % 4) for i in range(8)])


def x_low_swap(a):
    return lax.ppermute(a, "dp", [(i, (i + 4) % 8) for i in range(8)])


def y_shift(a, by):
    return lax.ppermute(a, "tm", [(i, (i + 4 * by) % 16) for i in range(16)])


def x_flip(a, flip_high, flip_low):
    pairs = []
    for tm in range(16):
        for dp in range(8):
            to_tm = tm ^ 2 if flip_high else tm
            to_dp = dp ^ 4 if flip_low else dp
            pairs.append((tm * 8 + dp, to_tm * 8 + to_dp))
    return lax.ppermute(a, ("tm", "dp"), pairs)


def project_kernel(place_ref, rows_ref, *refs):
    pieces, out_ref, held, sems = refs[:8], refs[8], refs[9], refs[10]
    z, core = place_ref[0], place_ref[1]
    copies = []
    for index, piece in enumerate(pieces):
        half = core if index < 4 else 1 - core
        source = lax.rem(z - index % 4 + 4, 4)
        for low in range(2):
            row = pl.multiple_of(low * 768 + source * 192 + half * 96, 96)
            copies.append(
                pltpu.make_async_copy(
                    piece.at[low], held.at[pl.ds(row, 96), :], sems.at[index, low]
                )
            )
    for copy in copies:
        copy.start()
    for copy in copies:
        copy.wait()

    @pl.loop(0, FEATURES // 256)
    def _(j):
        cols = pl.ds(pl.multiple_of(j * 256, 256), 256)
        out_ref[:, cols] = nn(rows_ref[...], held[:, cols]).astype(BF16)


def project(place, rows_in, pieces):
    return pl.pallas_call(
        project_kernel,
        out_shape=jax.ShapeDtypeStruct((ROWS, FEATURES), BF16),
        in_specs=[
            pl.BlockSpec(memory_space=pltpu.SMEM),
            pl.BlockSpec(memory_space=pltpu.VMEM),
        ]
        + [pl.BlockSpec(memory_space=pl.ANY)] * 8,
        out_specs=pl.BlockSpec(memory_space=pltpu.VMEM),
        scratch_shapes=[
            pltpu.VMEM((FEATURES, FEATURES), BF16),
            pltpu.SemaphoreType.DMA((8, 2)),
        ],
        compiler_params=pltpu.CompilerParams(vmem_limit_bytes=VMEM),
        cost_estimate=pl.CostEstimate(
            flops=ROWS * FEATURES, bytes_accessed=1_000_000, transcendentals=0
        ),
        name="project",
    )(place, rows_in, *pieces)


def attention_kernel(
    codes_ref, lens_ref, q_ref, g_ref, ko, vo, ki, vi, kvx, *refs
):
    dq_ref, att_ref, own_ref, in_ref, out_ref = refs[-11:-6]
    kp, vp, kt, vt, acck, accv = refs[-6:]
    for tile in range(TILES):
        part = slice(tile * TILE, (tile + 1) * TILE)
        for base, k, v in (
            (0, ko[part, :], vo[part, :]),
            (2, ki[part, :], vi[part, :]),
            (4, kvx[0, part, :], kvx[1, part, :]),
        ):
            kp[base + tile] = k
            vp[base + tile] = v
            kt[base + tile] = k.T
            vt[base + tile] = v.T
    acck[...] = jnp.zeros_like(acck)
    accv[...] = jnp.zeros_like(accv)
    place = lax.broadcasted_iota(jnp.int32, (TILE, TILE), 0)

    for tile in range(TILES):
        rows = slice(tile * TILE, (tile + 1) * TILE)
        q = q_ref[rows, :]
        g = g_ref[rows, :]
        codes = [codes_ref[tile, slot] for slot in range(SLOTS)]
        scores = []
        for slot in range(SLOTS):
            s = nt(kp[codes[slot]], q) * (SCALING * LOG2E)
            scores.append(jnp.where(place < lens_ref[tile, slot], s, -jnp.inf))
        top = functools.reduce(
            jnp.maximum, [jnp.max(s, axis=0, keepdims=True) for s in scores]
        )
        powers = [jnp.exp2(s - top) for s in scores]
        total = sum(jnp.sum(e, axis=0, keepdims=True) for e in powers)
        inverse = 1.0 / total
        probs = [e * inverse for e in powers]
        weights = [p.astype(BF16) for p in probs]
        every = jnp.concatenate(weights, axis=0)
        att = nn(jnp.concatenate([vt[code] for code in codes], axis=1), every).astype(BF16)
        att_ref[rows, :] = att.T
        rowdot = jnp.sum(g.T.astype(F32) * att.astype(F32), axis=0, keepdims=True)
        dscores = []
        for slot in range(SLOTS):
            code = codes[slot]
            prob_grad = nt(vp[code], g)
            dscore = (probs[slot] * (prob_grad - rowdot)).astype(BF16)
            dscores.append(dscore)
            acck[code] += nn(dscore, q)
            accv[code] += nn(weights[slot], g)
        every = jnp.concatenate(dscores, axis=0)
        dq = nn(jnp.concatenate([kt[code] for code in codes], axis=1), every)
        dq_ref[rows, :] = (dq * SCALING).astype(BF16).T

    for tile in range(TILES):
        part = slice(tile * TILE, (tile + 1) * TILE)
        for base, ref in ((0, own_ref), (2, in_ref), (4, out_ref)):
            ref[0, part, :] = (acck[base + tile] * SCALING).astype(ref.dtype)
            ref[1, part, :] = accv[base + tile].astype(ref.dtype)


def attention(codes, lens, q, g, ko, vo, ki, vi, kvx, first, skip, heads, inside, held, width):
    at_head = pl.BlockSpec((ROWS, HEAD), lambda i: (0, first + i))
    pair = pl.BlockSpec((2, ROWS, HEAD), lambda i: (0, 0, skip + i))
    part = pl.BlockSpec((2, ROWS, HEAD), lambda i: (0, 0, inside + i))
    smem = pl.BlockSpec(memory_space=pltpu.SMEM)
    operands = [codes, lens, q, g, ko, vo, ki, vi, kvx]
    in_specs = [smem, smem] + [at_head] * 6 + [pair]
    aliases = {}
    for index, array in enumerate(held):
        if array is not None:
            aliases[len(operands)] = index
            operands.append(array)
            in_specs.append(pl.BlockSpec(memory_space=pl.ANY))
    at_half = pl.BlockSpec((ROWS, HEAD), lambda i: (0, first % 6 + i))
    macs = 6 * heads * TILES * TILE * SLOTS * TILE * HEAD
    return pl.pallas_call(
        attention_kernel,
        grid=(heads,),
        out_shape=[
            jax.ShapeDtypeStruct((ROWS, FEATURES), BF16),
            jax.ShapeDtypeStruct((ROWS, HALF), BF16),
            jax.ShapeDtypeStruct((2, ROWS, width), F32),
            jax.ShapeDtypeStruct((2, ROWS, width), BF16),
            jax.ShapeDtypeStruct((2, ROWS, width), BF16),
        ],
        in_specs=in_specs,
        out_specs=[at_head, at_half, part, part, part],
        scratch_shapes=[
            pltpu.VMEM((POOL, TILE, HEAD), BF16),
            pltpu.VMEM((POOL, TILE, HEAD), BF16),
            pltpu.VMEM((POOL, HEAD, TILE), BF16),
            pltpu.VMEM((POOL, HEAD, TILE), BF16),
            pltpu.VMEM((POOL, TILE, HEAD), F32),
            pltpu.VMEM((POOL, TILE, HEAD), F32),
        ],
        input_output_aliases=aliases,
        compiler_params=pltpu.CompilerParams(vmem_limit_bytes=VMEM),
        cost_estimate=pl.CostEstimate(
            flops=macs // 64, bytes_accessed=ROWS * width, transcendentals=0
        ),
        name="attention",
    )(*operands)


def finish_kernel(own_ref, in_ref, out_ref, *refs):
    for index, ref in enumerate(refs[-2:]):
        total = own_ref[index] + in_ref[index].astype(F32) + out_ref[index].astype(F32)
        ref[...] = total.astype(BF16)


def finish(own, from_in, from_out, first, held):
    width = own.shape[2]
    step = 384 if width % 384 == 0 else 256
    pair = pl.BlockSpec((2, ROWS, step), lambda i: (0, 0, i))
    place = pl.BlockSpec((ROWS, step), lambda i: (0, first * HEAD // step + i))
    whole = jax.ShapeDtypeStruct((ROWS, FEATURES), BF16)
    operands = [own, from_in, from_out] + list(held)
    return pl.pallas_call(
        finish_kernel,
        grid=(width // step,),
        out_shape=[whole, whole],
        in_specs=[pair] * 3 + [pl.BlockSpec(memory_space=pl.ANY)] * len(held),
        out_specs=[place, place],
        input_output_aliases={3 + i: i for i in range(len(held))},
        compiler_params=pltpu.CompilerParams(vmem_limit_bytes=VMEM),
        cost_estimate=pl.CostEstimate(
            flops=ROWS * width, bytes_accessed=ROWS * width, transcendentals=0
        ),
        name="finish",
    )(*operands)


def picked(array, axis, index):
    return lax.dynamic_index_in_dim(array, index, axis, keepdims=False)


def weight_kernel(core_ref, rows_ref, att_ref, keep_ref, send_ref, held):
    for part in range(4):
        rows = slice(part * 384, (part + 1) * 384)
        held[2 * part : 2 * part + 2] = nn(rows_ref[rows, :], att_ref[...]).reshape(2, 192, 256)
    for ref, core in ((keep_ref, core_ref[0]), (send_ref, 1 - core_ref[0])):
        rows = pl.ds(pl.multiple_of(core * 96, 96), 96)
        ref[...] = held[:, rows, :].astype(ref.dtype)


def weight_parts(core, rows_t, att):
    block = pl.BlockSpec((8, 96, 256), lambda i: (0, 0, i))
    return pl.pallas_call(
        weight_kernel,
        grid=(HALF // 256,),
        out_shape=[jax.ShapeDtypeStruct((8, 96, HALF), kind) for kind in (F32, BF16)],
        in_specs=[
            pl.BlockSpec(memory_space=pltpu.SMEM),
            pl.BlockSpec((FEATURES, ROWS), lambda i: (0, 0)),
            pl.BlockSpec((ROWS, 256), lambda i: (0, i)),
        ],
        out_specs=[block, block],
        scratch_shapes=[pltpu.VMEM((8, 192, 256), F32)],
        compiler_params=pltpu.CompilerParams(vmem_limit_bytes=VMEM),
        cost_estimate=pl.CostEstimate(
            flops=ROWS * HALF, bytes_accessed=500_000, transcendentals=0
        ),
        name="weight_parts",
    )(core, rows_t, att)


def core_sum_kernel(z_ref, keep_ref, got_ref, *refs):
    held = refs[4]
    for high in range(2):
        total = keep_ref[high] + got_ref[high].astype(F32)
        for low in range(2):
            for z in range(4):
                row, place = low * 48 + z * 12, (high * 2 + low) * 12
                by = lax.rem(z - z_ref[0] + 4, 4)
                held[by, place : place + 12, :] = total[row : row + 12, :]
    for by, ref in enumerate(refs[:4]):
        ref[...] = held[by].astype(ref.dtype)


def core_sum(z, keep, got):
    block = pl.BlockSpec((2, 96, HALF), lambda i: (i, 0, 0))
    return pl.pallas_call(
        core_sum_kernel,
        grid=(4,),
        out_shape=[jax.ShapeDtypeStruct((192, HALF), kind) for kind in (F32, BF16, BF16, BF16)],
        in_specs=[pl.BlockSpec(memory_space=pltpu.SMEM), block, block],
        out_specs=[pl.BlockSpec((48, HALF), lambda i: (i, 0))] * 4,
        scratch_shapes=[pltpu.VMEM((4, 48, HALF), F32)],
        compiler_params=pltpu.CompilerParams(vmem_limit_bytes=VMEM),
        cost_estimate=pl.CostEstimate(
            flops=ROWS * HALF, bytes_accessed=500_000, transcendentals=0
        ),
        name="core_sum",
    )(z, keep, got)


def z_sum_kernel(y_ref, *refs):
    outs, held = refs[8:12], refs[12]
    for side in range(2):
        own, got = refs[4 * side], refs[4 * side + 1 : 4 * side + 4]
        cols = slice(side * HALF, (side + 1) * HALF)
        held[:, cols] = own[...] + sum(ref[...].astype(F32) for ref in got)
    for by, ref in enumerate(outs):
        row = pl.multiple_of(lax.rem(y_ref[0] + by, 4) * 48, 48)
        ref[...] = held[pl.ds(row, 48), :].astype(ref.dtype)


def z_sum(y, sides):
    whole = pl.BlockSpec(memory_space=pltpu.VMEM)
    return pl.pallas_call(
        z_sum_kernel,
        out_shape=[jax.ShapeDtypeStruct((48, FEATURES), kind) for kind in (F32, BF16, BF16, BF16)],
        in_specs=[pl.BlockSpec(memory_space=pltpu.SMEM)] + [whole] * 8,
        out_specs=[whole] * 4,
        scratch_shapes=[pltpu.VMEM((192, FEATURES), F32)],
        compiler_params=pltpu.CompilerParams(vmem_limit_bytes=VMEM),
        cost_estimate=pl.CostEstimate(
            flops=ROWS * HALF, bytes_accessed=500_000, transcendentals=0
        ),
        name="z_sum",
    )(y, *sides)


def x_sum(held, tm, dp):
    x_high, x_low = (tm // 2) % 2, dp // 4
    got = []
    for high, low in ((0, 1), (1, 0), (1, 1)):
        to_high = x_high ^ 1 if high else x_high
        to_low = x_low ^ 1 if low else x_low
        block = picked(picked(held, 0, to_high), 0, to_low)
        got.append(x_flip(block.astype(BF16), high, low))
    own = picked(picked(held, 0, x_high), 0, x_low)
    return own + sum(a.astype(F32) for a in got)


def shards(queries, key_states, value_states, out_grad, out_weight, win_time, win_space, tile_len):
    tm, dp = lax.axis_index("tm"), lax.axis_index("dp")
    core, z = tm % 2, dp % 4
    q, k, v, rows_in = queries[0], key_states[0], value_states[0], out_grad[0]

    step = jnp.concatenate((jnp.zeros((TILES, 1), jnp.int32), win_time[0]), axis=1)
    own = lax.broadcasted_iota(jnp.int32, (TILES, 1), 0)
    space = jnp.concatenate((own, win_space[0]), axis=1)
    to_inner = (step == 1) == (core == 0)
    codes = jnp.where(step == 0, 0, jnp.where(to_inner, 2, 4)) + space
    named = ((tm + step + 16) % 16) * TILES + space
    chosen = named[:, :, None] == lax.broadcasted_iota(jnp.int32, (TILES, SLOTS, 32), 2)
    lens = jnp.sum(jnp.where(chosen, tile_len[0][None, None, :], 0), axis=2)

    starts = [sum(GROUPS[:i]) for i in range(len(GROUPS))]
    together = lax.optimization_barrier

    def outgoing(i):
        cols = slice(starts[i] * HEAD, (starts[i] + GROUPS[i]) * HEAD)
        return jnp.stack((k[:, cols], v[:, cols]))

    x_low = dp // 4
    half = lax.dynamic_slice_in_dim(out_weight, core * 96, 96, 0)
    leaving = [outgoing(i) for i in range(len(GROUPS))]
    other = jnp.concatenate((x_low_swap(half[:48]), x_flip(half[48:], 1, 1)), axis=0)
    leaving[0], other = together((leaving[0], other))
    arriving = [outer_swap(leaving[0])]
    both = jnp.stack((jnp.where(x_low == 0, half, other), jnp.where(x_low == 0, other, half)))
    mine = [both] + [z_shift(both, by) for by in (1, 2, 3)]
    leaving[1], mine[1] = together((leaving[1], mine[1]))
    arriving.append(outer_swap(leaving[1]))
    leaving[2], arriving[0] = together((leaving[2], arriving[0]))
    arriving.append(outer_swap(leaving[2]))
    ki, vi = inner_swap(k), inner_swap(v)
    rows_t = together((rows_in, both))[0].T
    ready, arriving[0], rows_t = together((tuple(mine), arriving[0], rows_t))
    theirs = [inner_swap(a) for a in ready]
    place = jnp.stack((z, core)).astype(jnp.int32)
    place, arriving[1] = together((place, arriving[1]))
    head_grad = project(place, rows_in, mine + theirs)


    held = [None] * 5
    inside, first, parts, firsts = 0, 0, [], []
    for group, skip, heads, which in CALLS:
        width = sum(call[2] for call in CALLS if call[3] == which) * HEAD
        if first == 6:
            att_a = held[1]
            held = [held[0]] + [None] * 4
        held = attention(
            codes, lens, q, head_grad, k, v, ki, vi, arriving[group],
            first, skip, heads, inside, held, width,
        )
        inside += heads
        first += heads
        if inside * HEAD == width:
            parts.append([held[2], inner_swap(held[3]), outer_swap(held[4])])
            firsts.append(first - inside)
            held = list(held[:2]) + [None] * 3
            inside = 0
    dq, att_b = held[:2]
    att_a, att_b = together((att_a, att_b))
    keep_a, send_a = weight_parts(place[1:], rows_t, att_a)
    sums_a = core_sum(place[:1], keep_a, inner_swap(send_a))
    side_a = [sums_a[0]] + [z_shift(sums_a[by], by) for by in (1, 2, 3)]
    keep_b, send_b = weight_parts(place[1:], rows_t, att_b)
    send_b, parts[0][2] = together((send_b, parts[0][2]))
    sums_b = core_sum(place[:1], keep_b, inner_swap(send_b))
    side_b = [sums_b[0]] + [z_shift(sums_b[by], by) for by in (1, 2, 3)]
    grads = finish(*parts[0], 0, ())
    side_a[0], *grads = together((side_a[0], *grads))
    sums = z_sum((tm // 4).astype(jnp.int32)[None], side_a + side_b)
    total = sums[0] + sum(y_shift(sums[by], by).astype(F32) for by in (1, 2, 3))
    total, parts[1][2] = together((total, parts[1][2]))
    weight_grad = x_sum(total.reshape(2, 2, 12, FEATURES), tm, dp)
    dk, dv = finish(*parts[1], firsts[1], grads)
    return dq[None], dk[None], dv[None], weight_grad


def solution(mesh):
    tokens = P("dp", "tm", None)
    in_specs = (tokens, tokens, tokens, tokens, P("dp", None), tokens, tokens, P("dp", None))
    out_specs = (tokens, tokens, tokens, P(("tm", "dp"), None))
    return jax.shard_map(shards, mesh=mesh, in_specs=in_specs, out_specs=out_specs, check_vma=False)
```
